512 devices in a mesh: rep: 8 (over x, z_hi), zero: 64 (over z_lo, y, core).
Axes of the slice: x: 4, y: 4, z: 16 (z_hi: 2, z_lo: 8; z = z_hi * 8 + z_lo), core: 2. Of those that a mesh axis runs over, the one named last changes fastest.
Arguments:
- pooled: bfloat16 [65536, 768], P(('rep', 'zero')), may hold values from -24 to 24
- text_embed: bfloat16 [65536, 768], P(('rep', 'zero')), may hold values from -6 to 6
- head_weight: bfloat16 [768, 768], P('zero'), may hold values from -0.21875 to 0.21875
- natural_exponent_factor: float32 [1], replicated, may hold values from 3.4 to 4
- logit_bias: float32 [1], replicated, may hold values from -10 to -8
Outputs:
- row_loss: float32 [65536], P(('rep', 'zero'))
- feat_grad: bfloat16 [65536, 768], P(('rep', 'zero'))
- weight_grad: float32 [768, 768], P('zero')
- scale_grads: float32 [2], replicated
The draws below stay inside these ranges and needn't reach their ends.
All inputs are finite; a program needn't handle non-finite values.
Results may differ from the reference program's by a relative error of at most 0.015.
Values may be sent and summed in bfloat16 or wider, within the bound.
A program may use at most 64 MiB of HBM per device.

```python
import jax
import jax.numpy as jnp
from jax import lax

D = 768
E = 768
IMG_DEV = 128
IMAGES = 65536
N_REP = 8
N_ZERO = 64


def spiked(drawn, key, source, target, blocks, factor):
    owner, partner = [(jnp.arange(drawn.shape[axis_at]) // (drawn.shape[axis_at] // blocks)).reshape([-1 if axis == axis_at else 1 for axis in range(drawn.ndim)]) for axis_at in (source, target)]
    chosen = jax.random.permutation(key, blocks)[partner]
    strong = (owner == chosen) | (owner == (partner + blocks // 2) % blocks)
    return jnp.where(strong, factor * drawn, drawn)


def block_levels(stream_key, extent, split, least, top_value):
    loudness = 1.0
    for dim, parts in split:
        heights = jax.random.uniform(jax.random.fold_in(jax.random.fold_in(stream_key, 6), dim), (parts,), jnp.float32, least / len(split), top_value / len(split))
        loudness = loudness * jnp.repeat(jnp.exp(heights), extent[dim] // parts).reshape((-1,) + (1,) * (len(extent) - 1 - dim))
    return loudness


def normal_values(stream_key, dims, width, most, shards=(), held_as=jnp.bfloat16):
    gain = block_levels(stream_key, dims, shards, -0.22, 0.18) if shards else 1.0
    entries = jax.random.normal(stream_key, dims, jnp.float32) * width * gain
    return jnp.minimum(jnp.maximum(entries, -most), most).astype(held_as)


def bell_draw_with(stream_key, shape, width, reach, shards, heavy, held_as=jnp.bfloat16):
    entries = width * jax.random.normal(stream_key, shape, jnp.float32)
    if shards:
        entries = entries * block_levels(stream_key, shape, shards, -0.22, 0.18)
    return jnp.clip(spiked(entries, jax.random.fold_in(stream_key, 3), *heavy), -reach, reach).astype(held_as)


def setup_inputs(seed: int = 0) -> dict:
    keys = jax.random.split(jax.random.key(seed), 6)
    return {
        "pooled": bell_draw_with(keys[0], (IMAGES, D), 1.0, 24.0, ((0, 512),), (0, 1, 256, 6.0)),
        "text_embed": normal_values(keys[1], (IMAGES, E), 1.0, 6.0, ((0, 512),)),
        "head_weight": normal_values(keys[2], (D, E), D ** -0.5, 0.21875, ((0, 64),)),
        "natural_exponent_factor": jnp.clip(jax.random.uniform(keys[3], (1,), jnp.float32, 3.4, 4.0), 3.4, 4.0),
        "logit_bias": jnp.clip(jax.random.uniform(keys[4], (1,), jnp.float32, -10.0, -8.0), -10.0, -8.0),
    }


def patch_penalty_entries(picture_sample_slab, caption_sample_slab, matching_pair_sign, inverse_warmth_factor, offset_count):
    cosine_matrix_entries = lax.dot_general(picture_sample_slab, caption_sample_slab, (((1,), (1,)), ((), ())), preferred_element_type=jnp.float32)
    multiplied_affinities = inverse_warmth_factor * cosine_matrix_entries
    logits = multiplied_affinities + offset_count
    polarity = jnp.where(matching_pair_sign, 1.0, -1.0).astype(jnp.float32)
    row_losses = lax.optimization_barrier(jnp.sum(jax.nn.softplus(-polarity * logits), axis=1))
    squashing_derivatives = -polarity * jax.nn.sigmoid(-polarity * logits)
    temp_total = jnp.sum(squashing_derivatives * multiplied_affinities)
    bias_total = jnp.sum(squashing_derivatives)
    upstream_derivative = inverse_warmth_factor * jnp.dot(squashing_derivatives.astype(jnp.bfloat16), caption_sample_slab, preferred_element_type=jnp.float32)
    return (row_losses, upstream_derivative, temp_total, bias_total)

def reference(pooled, text_embed, head_weight, natural_exponent_factor, logit_bias):
    inverse_warmth_factor = jnp.exp(natural_exponent_factor[0])
    offset_count = logit_bias[0]
    projected = jnp.dot(pooled, head_weight, preferred_element_type=jnp.float32)
    inverse = lax.rsqrt(lax.optimization_barrier(jnp.sum(projected * projected, axis=1, keepdims=True)) + 1e-06)
    img_unit = projected * inverse
    picture_bfloat_copy = img_unit.astype(jnp.bfloat16)
    text_float = text_embed.astype(jnp.float32)
    txt_bf = (text_float * lax.rsqrt(lax.optimization_barrier(jnp.sum(text_float * text_float, axis=1, keepdims=True)) + 1e-06)).astype(jnp.bfloat16)
    batch_rows = IMG_DEV
    group_rows = IMG_DEV * N_ZERO

    def block_terms(which):
        picture_sample_slab = lax.dynamic_slice_in_dim(picture_bfloat_copy, (which * batch_rows).astype(jnp.int32), batch_rows, 0)
        group_index = which // N_ZERO
        caption_sample_slab = lax.dynamic_slice_in_dim(txt_bf, (group_index * group_rows).astype(jnp.int32), group_rows, 0)
        mine = which % N_ZERO * batch_rows + jnp.arange(batch_rows, dtype=jnp.int32)
        columns = jnp.arange(group_rows, dtype=jnp.int32)
        matching_pair_sign = mine[:, None] == columns[None, :]
        return patch_penalty_entries(picture_sample_slab, caption_sample_slab, matching_pair_sign, inverse_warmth_factor, offset_count)
    row_losses, upstream_derivative, temp_totals, bias_totals = lax.map(block_terms, jnp.arange(N_REP * N_ZERO, dtype=jnp.int32))
    row_loss = row_losses.reshape(-1)
    grad_unit = upstream_derivative.reshape(-1, upstream_derivative.shape[-1])
    scale_grads = jnp.stack([jnp.sum(temp_totals), jnp.sum(bias_totals)])
    grad_proj = ((grad_unit - img_unit * lax.optimization_barrier(jnp.sum(img_unit * grad_unit, axis=1, keepdims=True))) * inverse).astype(jnp.bfloat16)
    feat_grad = lax.dot_general(grad_proj, head_weight, (((1,), (1,)), ((), ())), preferred_element_type=jnp.float32).astype(jnp.bfloat16)
    weight_grad = lax.dot_general(pooled, grad_proj, (((0,), (0,)), ((), ())), preferred_element_type=jnp.float32)
    return (row_loss, feat_grad, weight_grad, scale_grads)
```

```python
import jax
import jax.numpy as jnp
from jax import lax
from jax.experimental import pallas as pl
from jax.experimental.pallas import tpu as pltpu
from jax.sharding import PartitionSpec as P

MESH = pl.DeviceIdType.MESH
F32 = jnp.float32
BF = jnp.bfloat16


def dev(x, zh, zl, y, c):
    return (x * 2 + zh, zl * 8 + y * 2 + c)


def rem(a, n):
    return lax.rem(a, jnp.int32(n))


def div(a, n):
    return lax.div(a, jnp.int32(n))


def nn(a, b):
    return jnp.dot(a, b, preferred_element_type=F32)


def nt(a, b):
    return lax.dot_general(a, b, (((1,), (1,)), ((), ())), preferred_element_type=F32)


def kernel(
    p_ref, t_ref, w_ref, nat_ref, bias_ref,
    loss_ref, feat_ref, wg_ref, sc_ref,
    txt, pool, wgat, sel, selt, wc, pt, iu, inv, img, s_scr, slope_scr, acc, loss_acc, tot_acc,
    gp, fsend, frecv, lbuf, cs, cbuf, xs, xbuf, ysum, zs, zbuf, agb, abuf, s2buf, s3buf,
    t_rs, t_sr, t_sl, t_ss, p_rs, p_s, wz_rs, wz_s, wx_rs, wx_s, wy_rs, wy_s, wc_rs, wc_s,
    f_rs, f_s, l_rs, l_s, c_rs, c_s, x_rs, x_s, z_rs, z_s, a_rs, a_s, s2_rs, s2_s, s3_rs, s3_s,
):
    rep = lax.axis_index("rep")
    zero = lax.axis_index("zero")
    x, zh = div(rep, 2), rem(rep, 2)
    zl, y, c = div(zero, 8), rem(div(zero, 2), 4), rem(zero, 2)
    oc = 1 - c
    temp = jnp.exp(jnp.full((8, 128), nat_ref[0], F32))[0:1, 0:1]
    bias = bias_ref[0]

    def rc(src, dst, ss, rs, to):
        return pltpu.make_async_remote_copy(src, dst, ss, rs, device_id=to, device_id_type=MESH)

    bar = pltpu.get_barrier_semaphore()

    def sig(to):
        pl.semaphore_signal(bar, inc=1, device_id=to, device_id_type=MESH)

    wgat[y, c, zl] = jnp.zeros((16, 768), BF)
    wgat[y, c, zl, 0:12] = w_ref[...]
    sig(dev(x, zh, zl, y, oc))
    for k in (1, 2, 3):
        sig(dev(x, zh, zl, rem(y + k, 4), c))
        sig(dev(rem(x + k, 4), zh, zl, y, c))
        sig(dev(rem(x + k, 4), 1 - zh, zl, y, c))
    for k in range(1, 8):
        sig(dev(x, zh, rem(zl + k, 8), y, c))
    sig(dev(x, 1 - zh, zl, y, c))

    def ag_self(k):
        return (div(k, 4) == x) & (rem(div(k, 2), 2) == zh) & (x == y) & (rem(k, 2) == c)

    def ag_from_self(k):
        return (x == y) & (div(k, 4) == y) & (rem(div(k, 2), 2) == zh) & (rem(k, 2) == c)

    tf = t_ref[...].astype(F32)
    txt[zl, c] = (tf * lax.rsqrt(jnp.sum(tf * tf, axis=1, keepdims=True) + 1e-06)).astype(BF)
    pl.semaphore_wait(bar, 18)

    def tpiece(slot, cc, h):
        return txt.at[slot, cc, pl.ds(h * 64, 64)]

    def t_right(slot, h):
        return rc(tpiece(slot, c, h), tpiece(slot, c, h), t_sr.at[slot, h], t_rs.at[slot, c, h], dev(x, zh, zl + 1, y, c))

    def t_left(slot, h):
        return rc(tpiece(slot, c, h), tpiece(slot, c, h), t_sl.at[slot, h], t_rs.at[slot, c, h], dev(x, zh, zl - 1, y, c))

    def t_sib(slot, h):
        return rc(tpiece(slot, c, h), tpiece(slot, c, h), t_ss.at[slot, h], t_rs.at[slot, c, h], dev(x, zh, zl, y, oc))

    def t_wait(slot, cc, h):
        rc(tpiece(slot, cc, h), tpiece(slot, cc, h), t_ss.at[slot, h], t_rs.at[slot, cc, h], dev(x, zh, zl, y, oc)).wait_recv()

    def wz(k_to, slot):
        piece = wgat.at[y, c, slot, :, pl.ds(pl.multiple_of(x * 256, 256), 256)]
        return rc(piece, piece, wz_s.at[k_to], wz_rs.at[slot], dev(x, zh, k_to, y, c))

    def wx(xt, slot):
        piece = wgat.at[y, c, :, :, pl.ds(pl.multiple_of(slot * 256, 256), 256)]
        return rc(piece, piece, wx_s.at[xt], wx_rs.at[slot], dev(xt, zh, zl, y, c))

    def pcopy(yt, slot):
        return rc(p_ref, pool.at[slot], p_s.at[yt], p_rs.at[slot], dev(x, zh, zl, yt, c))

    @pl.when(x < 3)
    def _():
        for k in range(1, 8):
            wz(rem(zl + k, 8), zl).start()
    for h in (0, 1):
        @pl.when(zl < 7)
        def _():
            t_right(zl, h).start()

        @pl.when(zl > 0)
        def _():
            t_left(zl, h).start()
    for h in (0, 1):
        t_sib(zl, h).start()

    for k in (1, 3, 2):
        pcopy(rem(y + k, 4), y).start()

    def forward(d):
        pass
        for h in (0, 1):
            @pl.when(zl - d >= 0)
            def _():
                t_wait(zl - d, c, h)

                @pl.when(zl < 7)
                def _():
                    t_right(zl - d, h).start()
                t_sib(zl - d, h).start()

            @pl.when(zl + d <= 7)
            def _():
                t_wait(zl + d, c, h)

                @pl.when(zl > 0)
                def _():
                    t_left(zl + d, h).start()
                t_sib(zl + d, h).start()

    pool[y] = p_ref[...]

    def where_row(k):
        r = k % 16
        return jnp.where(r < 12, 96 * ((k // 16) % 8) + 12 * (k // 128) + r, -1)

    cols = where_row(lax.broadcasted_iota(jnp.int32, (1, 1024), 1))

    def body(i, _):
        rows = lax.broadcasted_iota(jnp.int32, (128, 1), 0) + i * 128
        sel[pl.ds(i * 128, 128), :] = jnp.where(rows == cols, 1.0, 0.0).astype(BF)
        return 0
    lax.fori_loop(0, 6, body, 0)
    lanes = lax.broadcasted_iota(jnp.int32, (1, 768), 1)

    def body(i, _):
        rows = where_row(lax.broadcasted_iota(jnp.int32, (128, 1), 0) + i * 128)
        selt[pl.ds(i * 128, 128), :] = jnp.where(rows == lanes, 1.0, 0.0).astype(BF)
        return 0
    lax.fori_loop(0, 8, body, 0)
    acc[...] = jnp.zeros_like(acc)
    loss_acc[...] = jnp.zeros_like(loss_acc)
    tot_acc[...] = jnp.zeros_like(tot_acc)
    @pl.when(x < 3)
    def _():
        for k in (1, 7, 2, 6, 3, 5, 4):
            wz(rem(zl + k, 8), rem(zl + k, 8)).wait_recv()
        for k in (1, 3, 2):
            wx(rem(x + k, 4), x).start()

    def wy(yt, slot):
        return rc(wgat.at[slot, c], wgat.at[slot, c], wy_s.at[yt], wy_rs.at[slot], dev(x, zh, zl, yt, c))

    def wcc(slot, cc):
        return rc(wgat.at[slot, cc], wgat.at[slot, cc], wc_s.at[slot], wc_rs.at[slot], dev(x, zh, zl, y, oc))

    forward(1)
    for k in range(3):
        @pl.when(x != k)
        def _():
            wx(0, k).wait_recv()
    for k in (1, 3, 2):
        wy(rem(y + k, 4), y).start()
    wcc(y, c).start()
    forward(2)
    for k in (1, 3, 2):
        pcopy(rem(y + k, 4), rem(y + k, 4)).wait_recv()

    def body(i, _):
        pt[pl.ds(i * 256, 256), :] = nt(selt[pl.ds(i * 256, 256), :], pool[...].reshape(512, 768)).astype(BF)
        return 0
    lax.fori_loop(0, 4, body, 0)
    forward(3)
    for k in (1, 3, 2):
        wy(rem(y + k, 4), rem(y + k, 4)).wait_recv()
        wcc(rem(y + k, 4), c).start()
    forward(4)
    for k in (0, 1, 3, 2):
        wcc(rem(y + k, 4), oc).wait_recv()

    def body(i, _):
        wc[pl.ds(i * 256, 256), :] = nn(sel[pl.ds(i * 256, 256), :], wgat[...].reshape(1024, 768)).astype(BF)
        return 0
    lax.fori_loop(0, 3, body, 0)
    for n in range(3):
        iu[:, n * 256:(n + 1) * 256] = nn(pool[...].reshape(512, 768), wc[:, n * 256:(n + 1) * 256])

    def body(i, _):
        rows = pl.ds(i * 64, 64)
        pr = iu[rows, :]
        iv = lax.rsqrt(jnp.sum(pr * pr, axis=1, keepdims=True) + 1e-06)
        un = pr * iv
        iu[rows, :] = un
        inv[rows, :] = iv
        img[rows, :] = un.astype(BF)
        return 0
    lax.fori_loop(0, 8, body, 0)

    def compute(slot, own):
        pass
        for h in (0, 1):
            t_wait(slot, oc, h)
        tt = txt[slot].reshape(256, 768)
        s_scr[...] = nt(img[...], tt)

        def body(i, _):
            rows = pl.ds(i * 64, 64)
            scaled = s_scr[rows, :] * temp
            logit = scaled + bias
            if own:
                diag = (
                    lax.broadcasted_iota(jnp.int32, (64, 256), 0) + (i * 64 - y * 128)
                    == lax.broadcasted_iota(jnp.int32, (64, 256), 1) - c * 128
                ) & (lax.broadcasted_iota(jnp.int32, (64, 256), 1) // 128 == c)
                m = jnp.where(diag, -logit, logit)
            else:
                m = logit
            e = jnp.exp(-jnp.abs(m))
            u = 1.0 + e
            rcp = 1.0 / u
            lg = jnp.log(u) + (e - (u - 1.0)) * rcp
            soft = jnp.maximum(m, 0.0) + lg
            slope = jnp.where(m >= 0.0, 1.0, e) * rcp
            if own:
                slope = jnp.where(diag, -slope, slope)
            loss_acc[rows, :] += soft[:, 0:128] + soft[:, 128:256]
            sl = slope[:, 0:128] + slope[:, 128:256]
            st = slope * scaled
            st = st[:, 0:128] + st[:, 128:256]
            tot_acc[0] += jnp.sum(st.reshape(8, 8, 128), axis=0)
            tot_acc[1] += jnp.sum(sl.reshape(8, 8, 128), axis=0)
            slope_scr[rows, :] = slope.astype(BF)
            return 0
        lax.fori_loop(0, 8, body, 0)
        for n in range(3):
            acc[:, n * 256:(n + 1) * 256] += nn(slope_scr[...], tt[:, n * 256:(n + 1) * 256])

    forward(5)
    compute(zl, True)

    def both(d):
        def body(side, _):
            slot = zl + d * (2 * side - 1)

            @pl.when((slot >= 0) & (slot <= 7))
            def _():
                compute(slot, False)
            return 0
        lax.fori_loop(0, 2, body, 0)

    def body(d, _):
        @pl.when(d == 3)
        def _():
            forward(6)

        @pl.when(d == 6)
        def _():
            forward(7)
        both(d)
        return 0
    lax.fori_loop(1, 8, body, 0)

    def body(i, _):
        rows = pl.ds(i * 64, 64)
        gu = acc[rows, :] * temp
        un = iu[rows, :]
        g = ((gu - un * jnp.sum(un * gu, axis=1, keepdims=True)) * inv[rows, :]).astype(BF)
        gp[0, rows, :] = g[:, 0:384]
        gp[1, rows, :] = g[:, 384:768]
        return 0
    lax.fori_loop(0, 8, body, 0)
    def cchunk(j):
        return rc(cs.at[j], cbuf.at[j], c_s.at[j], c_rs.at[j], dev(x, zh, zl, y, oc))

    def body(k, _):
        j = rem(x + k, 4)
        cs[j] = nn(pt[pl.ds(j * 256, 256), :], gp[oc]).astype(BF)
        cchunk(j).start()
        return 0
    lax.fori_loop(1, 5, body, 0)

    def zcopy(to, slot):
        return rc(zs.at[:, to], zbuf.at[slot], z_s.at[to], z_rs.at[slot], dev(x, zh, to, y, c))

    me_xy = x * 4 + y

    def xycopy(xt, n, slot):
        return rc(xs.at[xt, n], xbuf.at[slot], x_s.at[xt, n], x_rs.at[slot], dev(xt, zh, zl, n, c))

    def body(k, _):
        j = rem(x + k, 4)
        mine = nn(pt[pl.ds(j * 256, 256), :], gp[c])
        cchunk(j).wait_recv()
        both_ = mine + cbuf[j].astype(F32)
        for n in range(3):
            xs[j, n] = both_[:, n * 128:(n + 1) * 128].astype(BF)

            @pl.when((k < 4) | (y != n))
            def _():
                xycopy(j, n, me_xy).start()
        return 0
    lax.fori_loop(1, 5, body, 0)

    @pl.when(y < 3)
    def _():
        xbuf[me_xy] = xs[x, y]

    for n in range(3):
        blk = wc[n * 256:(n + 1) * 256, :]
        fsend[:, :, n * 256:(n + 1) * 256] = (
            (nt(gp[0], blk[:, 0:384]) + nt(gp[1], blk[:, 384:768])).astype(BF).reshape(4, 128, 256)
        )

    def fcopy(yt, slot):
        return rc(fsend.at[yt], frecv.at[slot], f_s.at[yt], f_rs.at[slot], dev(x, zh, zl, yt, c))

    row = lax.broadcasted_iota(jnp.int32, (8, 128), 0)
    tl = jnp.sum(tot_acc[0], axis=0, keepdims=True)
    bl = jnp.sum(tot_acc[1], axis=0, keepdims=True)
    for j in range(4):
        part = jnp.sum(loss_acc[j * 128:(j + 1) * 128, :].T, axis=0, keepdims=True)
        lbuf[0, j] = jnp.where(row == 0, part, jnp.where(row == 1, tl, jnp.where(row == 2, bl, 0.0)))

    def lcopy(yt, slot):
        return rc(lbuf.at[0, yt], lbuf.at[1, slot], l_s.at[yt], l_rs.at[slot], dev(x, zh, zl, yt, c))

    for k in (1, 2, 3):
        lcopy(rem(y + k, 4), y).start()
    lbuf[1, y] = lbuf[0, y]
    for k in (1, 2, 3):
        lcopy(rem(y + k, 4), rem(y + k, 4)).wait_recv()
    ltot = lbuf[1, 0] + lbuf[1, 1] + lbuf[1, 2] + lbuf[1, 3]
    loss_ref[...] = ltot[0]
    me2 = zl * 2 + c
    s2buf[me2] = ltot

    def s2(to, slot):
        return rc(s2buf.at[me2], s2buf.at[slot], s2_s.at[to], s2_rs.at[slot], dev(x, zh, div(to, 2), y, rem(to, 2)))

    for k in range(1, 16):
        s2(rem(me2 + k, 16), me2).start()

    @pl.when(y < 3)
    def _():
        for k in range(1, 16):
            xycopy(0, 0, rem(me_xy + k, 16)).wait_recv()

        def body(i, _):
            rows = pl.ds(i * 64, 64)
            part = xbuf[0, rows, :].astype(F32)
            for k in range(1, 16):
                part = part + xbuf[k, rows, :].astype(F32)
            ysum[rows, :] = part.astype(BF)
            return 0
        lax.fori_loop(0, 4, body, 0)
        zs[...] = ysum[...].reshape(2, 8, 16, 128)
        for k in (4, 3, 5, 2, 6, 1, 7):
            zcopy(rem(zl + k, 8), zl).start()

    for k in (2, 1, 3):
        fcopy(rem(y + k, 4), y).start()

    for k in range(1, 16):
        s2(rem(me2 + k, 16), rem(me2 + k, 16)).wait_recv()
    s3buf[rep] = jnp.sum(s2buf[...], axis=0)

    def s3(to, slot):
        return rc(s3buf.at[rep], s3buf.at[slot], s3_s.at[to], s3_rs.at[slot], (to, zero))

    for k in range(1, 8):
        s3(rem(rep + k, 8), rep).start()

    def acopy(k, j, h):
        return rc(
            agb.at[rem(k, 2)], abuf.at[h, j], a_s.at[k], a_rs.at[h, j],
            dev(div(k, 4), rem(div(k, 2), 2), zl, x, rem(k, 2)),
        )

    me_a = c * 3 + y

    @pl.when(y < 3)
    def _():
        zbuf[zl] = zs[:, zl]
        for k in (1, 7, 2, 6, 3, 5, 4):
            zcopy(rem(zl + k, 8), rem(zl + k, 8)).wait_recv()
        agb[...] = jnp.sum(zbuf[...].astype(F32), axis=0).astype(BF)

        def body(k, _):
            @pl.when(jnp.logical_not(ag_self(k)))
            def _():
                acopy(k, me_a, zh).start()
            return 0
        lax.fori_loop(0, 16, body, 0)

        @pl.when(x == y)
        def _():
            abuf[zh, me_a] = agb[c]

    for k in (1, 3, 2):
        fcopy(rem(y + k, 4), rem(y + k, 4)).wait_recv()
    frecv[y] = fsend[y]
    feat_ref[...] = (
        frecv[0].astype(F32) + frecv[1].astype(F32) + frecv[2].astype(F32) + frecv[3].astype(F32)
    ).astype(BF)

    for k in range(1, 8):
        s3(rem(rep + k, 8), rem(rep + k, 8)).wait_recv()
    fin = jnp.sum(s3buf[...], axis=0)
    sc_ref[0] = jnp.sum(fin[1:2, :])
    sc_ref[1] = jnp.sum(fin[2:3, :])

    @pl.when(x < 3)
    def _():
        for k in range(1, 8):
            wz(rem(zl + k, 8), zl).wait_send()
        for k in (1, 2, 3):
            wx(rem(x + k, 4), x).wait_send()
    for k in (1, 2, 3):
        pass
        pcopy(rem(y + k, 4), y).wait_send()
        wy(rem(y + k, 4), y).wait_send()
        fcopy(rem(y + k, 4), y).wait_send()
        lcopy(rem(y + k, 4), y).wait_send()
    for n in range(3):
        for k in (1, 2, 3):
            xycopy(rem(x + k, 4), n, me_xy).wait_send()

        @pl.when(y != n)
        def _():
            xycopy(x, n, me_xy).wait_send()
    for k in range(4):
        pass
        wcc(k, c).wait_send()
        cchunk(k).wait_send()

    def body(slot, _):
        for h in (0, 1):
            t_sib(slot, h).wait_send()

            @pl.when((slot <= zl) & (zl < 7))
            def _():
                t_right(slot, h).wait_send()

            @pl.when((slot >= zl) & (zl > 0))
            def _():
                t_left(slot, h).wait_send()
        return 0
    lax.fori_loop(0, 8, body, 0)
    for k in range(1, 16):
        s2(rem(me2 + k, 16), me2).wait_send()
    for k in range(1, 8):
        s3(rem(rep + k, 8), rep).wait_send()

    @pl.when(y < 3)
    def _():
        for k in range(1, 8):
            zcopy(rem(zl + k, 8), zl).wait_send()

    def body(k, _):
        @pl.when(jnp.logical_not(ag_from_self(k)))
        def _():
            acopy(0, rem(k, 2) * 3 + div(k, 4), rem(div(k, 2), 2)).wait_recv()
        return 0
    lax.fori_loop(0, 12, body, 0)
    for j in range(6):
        wg_ref[:, j * 128:(j + 1) * 128] = (abuf[0, j].astype(F32) + abuf[1, j].astype(F32))[0:12, :]

    @pl.when(y < 3)
    def _():
        def body(k, _):
            @pl.when(jnp.logical_not(ag_self(k)))
            def _():
                acopy(k, me_a, zh).wait_send()
            return 0
        lax.fori_loop(0, 16, body, 0)


def hand_out(loss_in, feat_in, wg_in, sc_in, loss_out, feat_out, wg_out, sc_out):
    loss_out[...] = loss_in[...]
    feat_out[...] = feat_in[...]
    wg_out[...] = wg_in[...]
    sc_out[0] = sc_in[0]
    sc_out[1] = sc_in[1]


def per_device(pooled, text_embed, head_weight, natural_exponent_factor, logit_bias):
    vm = pl.BlockSpec(memory_space=pltpu.VMEM)
    sm = pl.BlockSpec(memory_space=pltpu.SMEM)
    V = pltpu.VMEM
    D = pltpu.SemaphoreType.DMA
    loss, feat, wgrad, sc = pl.pallas_call(
        kernel,
        out_shape=(
            jax.ShapeDtypeStruct((128,), F32),
            jax.ShapeDtypeStruct((128, 768), BF),
            jax.ShapeDtypeStruct((12, 768), F32),
            jax.ShapeDtypeStruct((2,), F32),
        ),
        in_specs=[vm, vm, vm, sm, sm],
        out_specs=(vm, vm, vm, sm),
        scratch_shapes=[
            V((8, 2, 128, 768), BF), V((4, 128, 768), BF), V((4, 2, 8, 16, 768), BF),
            V((768, 1024), BF), V((1024, 768), BF), V((768, 768), BF), V((1024, 512), BF),
            V((512, 768), F32), V((512, 1), F32), V((512, 768), BF), V((512, 256), F32), V((512, 256), BF),
            V((512, 768), F32), V((512, 128), F32), V((2, 8, 128), F32),
            V((2, 512, 384), BF), V((4, 128, 768), BF), V((4, 128, 768), BF), V((2, 4, 8, 128), F32),
            V((4, 256, 384), BF), V((4, 256, 384), BF), V((4, 3, 256, 128), BF), V((16, 256, 128), BF), V((256, 128), BF),
            V((2, 8, 16, 128), BF), V((8, 2, 16, 128), BF), V((2, 16, 128), BF), V((2, 6, 16, 128), BF),
            V((16, 8, 128), F32), V((8, 8, 128), F32),
            D((8, 2, 2)), D((8, 2)), D((8, 2)), D((8, 2)), D((4,)), D((4,)),
            D((8,)), D((8,)), D((4,)), D((4,)), D((4,)), D((4,)), D((4,)), D((4,)),
            D((4,)), D((4,)), D((4,)), D((4,)), D((4,)), D((4,)), D((16,)), D((4, 3)),
            D((8,)), D((8,)), D((2, 6)), D((16,)), D((16,)), D((16,)), D((8,)), D((8,)),
        ],
        compiler_params=pltpu.CompilerParams(
            collective_id=0, has_side_effects=True, vmem_limit_bytes=56 << 20
        ),
    )(pooled, text_embed, head_weight, natural_exponent_factor, logit_bias)
    return pl.pallas_call(
        hand_out,
        out_shape=(
            jax.ShapeDtypeStruct((128,), F32),
            jax.ShapeDtypeStruct((128, 768), BF),
            jax.ShapeDtypeStruct((12, 768), F32),
            jax.ShapeDtypeStruct((2,), F32),
        ),
        in_specs=[vm, vm, vm, sm],
        out_specs=(vm, vm, vm, sm),
    )(loss, feat, wgrad, sc)


def solution(mesh):
    return jax.shard_map(
        per_device,
        mesh=mesh,
        in_specs=(P(("rep", "zero"), None), P(("rep", "zero"), None), P("zero", None), P(), P()),
        out_specs=(P(("rep", "zero")), P(("rep", "zero"), None), P("zero", None), P()),
        check_vma=False,
    )
```

```python
import jax
import jax.numpy as jnp
from jax import lax
from jax.experimental import pallas as pl
from jax.experimental.pallas import tpu as pltpu
from jax.sharding import PartitionSpec as P

MESH = pl.DeviceIdType.MESH
F32 = jnp.float32
BF = jnp.bfloat16


def dev(x, zh, zl, y, c):
    return (x * 2 + zh, zl * 8 + y * 2 + c)


def rem(a, n):
    return lax.rem(a, jnp.int32(n))


def div(a, n):
    return lax.div(a, jnp.int32(n))


def nn(a, b):
    return jnp.dot(a, b, preferred_element_type=F32)


def nt(a, b):
    return lax.dot_general(a, b, (((1,), (1,)), ((), ())), preferred_element_type=F32)


def kernel(
    p_ref, t_ref, w_ref, nat_ref, bias_ref,
    loss_ref, feat_ref, wg_ref, sc_ref,
    txt, pool, wgat, w2, sel, selt, wc, pt, iu, inv, img, s_scr, slope_scr, acc, loss_acc, tot_acc,
    gp, fsend, frecv, lbuf, cs, cbuf, xs, xbuf, ys, ybuf, ysum, zs, zbuf, agb, abuf, s2buf, s3buf,
    t_rs, t_sr, t_sl, t_ss, p_rs, p_s, wz_rs, wz_s, wx_rs, wx_s, wy_rs, wy_s, wc_rs, wc_s,
    f_rs, f_s, l_rs, l_s, c_rs, c_s, x_rs, x_s, y_rs, y_s, z_rs, z_s, a_rs, a_s, s2_rs, s2_s, s3_rs, s3_s,
):
    rep = lax.axis_index("rep")
    zero = lax.axis_index("zero")
    x, zh = div(rep, 2), rem(rep, 2)
    zl, y, c = div(zero, 8), rem(div(zero, 2), 4), rem(zero, 2)
    oc = 1 - c
    temp = jnp.exp(jnp.full((8, 128), nat_ref[0], F32))[0:1, 0:1]
    bias = bias_ref[0]

    def rc(src, dst, ss, rs, to):
        return pltpu.make_async_remote_copy(src, dst, ss, rs, device_id=to, device_id_type=MESH)

    bar = pltpu.get_barrier_semaphore()

    def sig(to):
        pl.semaphore_signal(bar, inc=1, device_id=to, device_id_type=MESH)

    wgat[y, c, zl] = jnp.zeros((16, 768), BF)
    wgat[y, c, zl, 0:12] = w_ref[...]
    sig(dev(x, zh, zl, y, oc))
    for k in (1, 2, 3):
        sig(dev(x, zh, zl, rem(y + k, 4), c))
        sig(dev(rem(x + k, 4), zh, zl, y, c))
        sig(dev(rem(x + k, 4), 1 - zh, zl, y, c))
    for k in range(1, 8):
        sig(dev(x, zh, rem(zl + k, 8), y, c))
    sig(dev(x, 1 - zh, zl, y, c))

    tf = t_ref[...].astype(F32)
    txt[zl, c] = (tf * lax.rsqrt(jnp.sum(tf * tf, axis=1, keepdims=True) + 1e-06)).astype(BF)
    pl.semaphore_wait(bar, 18)

    def tpiece(slot, cc, h):
        return txt.at[slot, cc, pl.ds(h * 64, 64)]

    def t_right(slot, h):
        return rc(tpiece(slot, c, h), tpiece(slot, c, h), t_sr.at[slot, h], t_rs.at[slot, c, h], dev(x, zh, zl + 1, y, c))

    def t_left(slot, h):
        return rc(tpiece(slot, c, h), tpiece(slot, c, h), t_sl.at[slot, h], t_rs.at[slot, c, h], dev(x, zh, zl - 1, y, c))

    def t_sib(slot, h):
        return rc(tpiece(slot, c, h), tpiece(slot, c, h), t_ss.at[slot, h], t_rs.at[slot, c, h], dev(x, zh, zl, y, oc))

    def t_wait(slot, cc, h):
        rc(tpiece(slot, cc, h), tpiece(slot, cc, h), t_ss.at[slot, h], t_rs.at[slot, cc, h], dev(x, zh, zl, y, oc)).wait_recv()

    def wz(k_to, slot):
        piece = wgat.at[y, c, slot, :, pl.ds(pl.multiple_of(x * 256, 256), 256)]
        return rc(piece, piece, wz_s.at[k_to], wz_rs.at[slot], dev(x, zh, k_to, y, c))

    def wx(xt, slot):
        piece = wgat.at[y, c, :, :, pl.ds(pl.multiple_of(slot * 256, 256), 256)]
        return rc(piece, piece, wx_s.at[xt], wx_rs.at[slot], dev(xt, zh, zl, y, c))

    def pcopy(yt, slot):
        return rc(p_ref, pool.at[slot], p_s.at[yt], p_rs.at[slot], dev(x, zh, zl, yt, c))

    @pl.when(x < 3)
    def _():
        for k in range(1, 8):
            wz(rem(zl + k, 8), zl).start()
    for h in (0, 1):
        @pl.when(zl < 7)
        def _():
            t_right(zl, h).start()

        @pl.when(zl > 0)
        def _():
            t_left(zl, h).start()
    for h in (0, 1):
        t_sib(zl, h).start()

    for k in (1, 3, 2):
        pcopy(rem(y + k, 4), y).start()

    def forward(d):
        pass
        for h in (0, 1):
            @pl.when(zl - d >= 0)
            def _():
                t_wait(zl - d, c, h)

                @pl.when(zl < 7)
                def _():
                    t_right(zl - d, h).start()
                t_sib(zl - d, h).start()

            @pl.when(zl + d <= 7)
            def _():
                t_wait(zl + d, c, h)

                @pl.when(zl > 0)
                def _():
                    t_left(zl + d, h).start()
                t_sib(zl + d, h).start()

    pool[y] = p_ref[...]

    def where_row(k):
        r = k % 16
        return jnp.where(r < 12, 96 * ((k // 16) % 8) + 12 * (k // 128) + r, -1)

    slots = lax.broadcasted_iota(jnp.int32, (1, 128), 1)
    slots = jnp.where(slots % 16 < 12, 12 * (slots // 16) + slots % 16, -1)
    csel = jnp.where(lax.broadcasted_iota(jnp.int32, (96, 1), 0) == slots, 1.0, 0.0).astype(BF)
    cols = lax.broadcasted_iota(jnp.int32, (1, 768), 1)
    cols = 96 * ((cols % 96) // 12) + 12 * (cols // 96) + cols % 12

    def body(i, _):
        rows = lax.broadcasted_iota(jnp.int32, (128, 1), 0) + i * 128
        sel[pl.ds(i * 128, 128), :] = jnp.where(rows == cols, 1.0, 0.0).astype(BF)
        return 0
    lax.fori_loop(0, 6, body, 0)
    lanes = lax.broadcasted_iota(jnp.int32, (1, 768), 1)

    def body(i, _):
        rows = where_row(lax.broadcasted_iota(jnp.int32, (128, 1), 0) + i * 128)
        selt[pl.ds(i * 128, 128), :] = jnp.where(rows == lanes, 1.0, 0.0).astype(BF)
        return 0
    lax.fori_loop(0, 8, body, 0)
    acc[...] = jnp.zeros_like(acc)
    loss_acc[...] = jnp.zeros_like(loss_acc)
    tot_acc[...] = jnp.zeros_like(tot_acc)
    @pl.when(x < 3)
    def _():
        for k in (1, 7, 2, 6, 3, 5, 4):
            wz(rem(zl + k, 8), rem(zl + k, 8)).wait_recv()
        for k in (1, 3, 2):
            wx(rem(x + k, 4), x).start()

    def wy(yt, slot):
        return rc(w2.at[slot, c], w2.at[slot, c], wy_s.at[yt], wy_rs.at[slot], dev(x, zh, zl, yt, c))

    def wcc(slot, cc):
        return rc(w2.at[slot, cc], w2.at[slot, cc], wc_s.at[slot], wc_rs.at[slot], dev(x, zh, zl, y, oc))

    forward(1)
    for k in range(3):
        @pl.when(x != k)
        def _():
            wx(0, k).wait_recv()
    w2[y, c] = nn(csel, wgat[y, c].reshape(128, 768)).astype(BF)
    for k in (1, 3, 2):
        wy(rem(y + k, 4), y).start()
    wcc(y, c).start()
    forward(2)
    for k in (1, 3, 2):
        pcopy(rem(y + k, 4), rem(y + k, 4)).wait_recv()

    def body(i, _):
        pt[pl.ds(i * 256, 256), :] = nt(selt[pl.ds(i * 256, 256), :], pool[...].reshape(512, 768)).astype(BF)
        return 0
    lax.fori_loop(0, 4, body, 0)
    forward(3)
    for k in (1, 3, 2):
        wy(rem(y + k, 4), rem(y + k, 4)).wait_recv()
        wcc(rem(y + k, 4), c).start()
    for k in (0, 1, 3, 2):
        wcc(rem(y + k, 4), oc).wait_recv()

    def body(i, _):
        wc[pl.ds(i * 256, 256), :] = nn(sel[pl.ds(i * 256, 256), :], w2[...].reshape(768, 768)).astype(BF)
        return 0
    lax.fori_loop(0, 3, body, 0)
    for n in range(3):
        iu[:, n * 256:(n + 1) * 256] = nn(pool[...].reshape(512, 768), wc[:, n * 256:(n + 1) * 256])

    def body(i, _):
        rows = pl.ds(i * 64, 64)
        pr = iu[rows, :]
        iv = lax.rsqrt(jnp.sum(pr * pr, axis=1, keepdims=True) + 1e-06)
        un = pr * iv
        iu[rows, :] = un
        inv[rows, :] = iv
        img[rows, :] = un.astype(BF)
        return 0
    lax.fori_loop(0, 8, body, 0)

    def compute(slot, own):
        pass
        for h in (0, 1):
            t_wait(slot, oc, h)
        tt = txt[slot].reshape(256, 768)
        s_scr[...] = nt(img[...], tt)

        def body(i, _):
            rows = pl.ds(i * 64, 64)
            scaled = s_scr[rows, :] * temp
            logit = scaled + bias
            if own:
                diag = (
                    lax.broadcasted_iota(jnp.int32, (64, 256), 0) + (i * 64 - y * 128)
                    == lax.broadcasted_iota(jnp.int32, (64, 256), 1) - c * 128
                ) & (lax.broadcasted_iota(jnp.int32, (64, 256), 1) // 128 == c)
                m = jnp.where(diag, -logit, logit)
            else:
                m = logit
            e = jnp.exp(-jnp.abs(m))
            u = 1.0 + e
            rcp = 1.0 / u
            lg = jnp.log(u) + (e - (u - 1.0)) * rcp
            soft = jnp.maximum(m, 0.0) + lg
            slope = jnp.where(m >= 0.0, 1.0, e) * rcp
            if own:
                slope = jnp.where(diag, -slope, slope)
            loss_acc[rows, :] += soft[:, 0:128] + soft[:, 128:256]
            sl = slope[:, 0:128] + slope[:, 128:256]
            st = slope * scaled
            st = st[:, 0:128] + st[:, 128:256]
            tot_acc[0] += jnp.sum(st.reshape(8, 8, 128), axis=0)
            tot_acc[1] += jnp.sum(sl.reshape(8, 8, 128), axis=0)
            slope_scr[rows, :] = slope.astype(BF)
            return 0
        lax.fori_loop(0, 8, body, 0)
        for n in range(3):
            acc[:, n * 256:(n + 1) * 256] += nn(slope_scr[...], tt[:, n * 256:(n + 1) * 256])

    forward(4)
    compute(zl, True)

    def both(d):
        def body(side, _):
            slot = zl + d * (2 * side - 1)

            @pl.when((slot >= 0) & (slot <= 7))
            def _():
                compute(slot, False)
            return 0
        lax.fori_loop(0, 2, body, 0)

    def body(d, _):
        @pl.when((d == 2) | (d == 4) | (d == 7))
        def _():
            forward(jnp.where(d == 2, 5, jnp.where(d == 4, 6, 7)))
        both(d)
        return 0
    lax.fori_loop(1, 8, body, 0)

    def body(i, _):
        rows = pl.ds(i * 64, 64)
        gu = acc[rows, :] * temp
        un = iu[rows, :]
        g = ((gu - un * jnp.sum(un * gu, axis=1, keepdims=True)) * inv[rows, :]).astype(BF)
        gp[0, rows, :] = g[:, 0:384]
        gp[1, rows, :] = g[:, 384:768]
        return 0
    lax.fori_loop(0, 8, body, 0)
    def cchunk(j):
        return rc(cs.at[j], cbuf.at[j], c_s.at[j], c_rs.at[j], dev(x, zh, zl, y, oc))

    def body(k, _):
        j = rem(jnp.where(c == 0, y, x) + k, 4)
        cs[j] = nn(pt[pl.ds(j * 256, 256), :], gp[oc]).astype(BF)
        cchunk(j).start()
        return 0
    lax.fori_loop(1, 5, body, 0)

    def zcopy(to, slot):
        return rc(zs.at[:, to], zbuf.at[slot], z_s.at[to], z_rs.at[slot], dev(x, zh, to, y, c))

    fst, snd = jnp.where(c == 0, x, y), jnp.where(c == 0, y, x)

    def place(f, g):
        return dev(jnp.where(c == 0, f, g), zh, zl, jnp.where(c == 0, g, f), c)

    def xcopy(to, slot):
        return rc(xs.at[to], xbuf.at[slot], x_s.at[to], x_rs.at[slot], place(to, snd))

    def ycopy(to, slot):
        return rc(ys.at[to], ybuf.at[slot], y_s.at[to], y_rs.at[slot], place(fst, to))

    def body(k, _):
        j = rem(fst + k, 4)
        mine = nn(pt[pl.ds(j * 256, 256), :], gp[c])
        cchunk(j).wait_recv()
        xs[j] = (mine + cbuf[j].astype(F32)).astype(BF)

        @pl.when(k < 4)
        def _():
            xcopy(j, fst).start()
        return 0
    lax.fori_loop(1, 5, body, 0)
    xbuf[fst] = xs[fst]

    for n in range(3):
        blk = wc[n * 256:(n + 1) * 256, :]
        fsend[:, :, n * 256:(n + 1) * 256] = (
            (nt(gp[0], blk[:, 0:384]) + nt(gp[1], blk[:, 384:768])).astype(BF).reshape(4, 128, 256)
        )

    def fcopy(yt, slot):
        return rc(fsend.at[yt], frecv.at[slot], f_s.at[yt], f_rs.at[slot], dev(x, zh, zl, yt, c))

    row = lax.broadcasted_iota(jnp.int32, (8, 128), 0)
    tl = jnp.sum(tot_acc[0], axis=0, keepdims=True)
    bl = jnp.sum(tot_acc[1], axis=0, keepdims=True)
    for j in range(4):
        part = jnp.sum(loss_acc[j * 128:(j + 1) * 128, :].T, axis=0, keepdims=True)
        lbuf[0, j] = jnp.where(row == 0, part, jnp.where(row == 1, tl, jnp.where(row == 2, bl, 0.0)))

    def lcopy(yt, slot):
        return rc(lbuf.at[0, yt], lbuf.at[1, slot], l_s.at[yt], l_rs.at[slot], dev(x, zh, zl, yt, c))

    for k in (1, 2, 3):
        lcopy(rem(y + k, 4), y).start()
    lbuf[1, y] = lbuf[0, y]
    for k in (1, 2, 3):
        lcopy(rem(y + k, 4), rem(y + k, 4)).wait_recv()
    ltot = lbuf[1, 0] + lbuf[1, 1] + lbuf[1, 2] + lbuf[1, 3]
    loss_ref[...] = ltot[0]
    me2 = zl * 2 + c
    s2buf[me2] = ltot

    def s2(to, slot):
        return rc(s2buf.at[me2], s2buf.at[slot], s2_s.at[to], s2_rs.at[slot], dev(x, zh, div(to, 2), y, rem(to, 2)))

    for k in range(1, 16):
        s2(rem(me2 + k, 16), me2).start()

    for k in (1, 3, 2):
        xcopy(0, rem(fst + k, 4)).wait_recv()

    def body(i, _):
        rows = pl.ds(i * 64, 64)
        part = xbuf[0, rows, :].astype(F32)
        for k in range(1, 4):
            part = part + xbuf[k, rows, :].astype(F32)
        for n in range(3):
            ys[n, rows, :] = part[:, n * 128:(n + 1) * 128].astype(BF)
        return 0
    lax.fori_loop(0, 4, body, 0)
    for n in range(3):
        @pl.when(snd != n)
        def _():
            ycopy(n, snd).start()
    for k in (2, 1, 3):
        fcopy(rem(y + k, 4), y).start()

    @pl.when(snd < 3)
    def _():
        ybuf[snd] = ys[snd]
        for k in (1, 3, 2):
            ycopy(0, rem(snd + k, 4)).wait_recv()
        ysum[...] = (
            ybuf[0].astype(F32) + ybuf[1].astype(F32) + ybuf[2].astype(F32) + ybuf[3].astype(F32)
        ).astype(BF)
        zs[...] = ysum[...].reshape(2, 8, 16, 128)
        for k in (4, 3, 5, 2, 6, 1, 7):
            zcopy(rem(zl + k, 8), zl).start()


    for k in range(1, 16):
        s2(rem(me2 + k, 16), rem(me2 + k, 16)).wait_recv()
    s3buf[rep] = jnp.sum(s2buf[...], axis=0)

    def s3(to, slot):
        return rc(s3buf.at[rep], s3buf.at[slot], s3_s.at[to], s3_rs.at[slot], (to, zero))

    for k in range(1, 8):
        s3(rem(rep + k, 8), rep).start()

    def ag_self(k):
        return (div(k, 4) == x) & (rem(div(k, 2), 2) == zh) & (fst == y) & (rem(k, 2) == c)

    def ag_from_self(k):
        return (fst == y) & (div(k, 4) == snd) & (rem(div(k, 2), 2) == zh) & (rem(k, 2) == c)

    def acopy(k, j, h):
        return rc(
            agb.at[rem(k, 2)], abuf.at[h, j], a_s.at[k], a_rs.at[h, j],
            dev(div(k, 4), rem(div(k, 2), 2), zl, fst, rem(k, 2)),
        )

    me_a = c * 3 + snd

    @pl.when(snd < 3)
    def _():
        zbuf[zl] = zs[:, zl]
        for k in (1, 7, 2, 6, 3, 5, 4):
            zcopy(rem(zl + k, 8), rem(zl + k, 8)).wait_recv()
        agb[...] = jnp.sum(zbuf[...].astype(F32), axis=0).astype(BF)

        def body(k, _):
            @pl.when(jnp.logical_not(ag_self(k)))
            def _():
                acopy(k, me_a, zh).start()
            return 0
        lax.fori_loop(0, 16, body, 0)

        @pl.when(fst == y)
        def _():
            abuf[zh, me_a] = agb[c]

    for k in (1, 3, 2):
        fcopy(rem(y + k, 4), rem(y + k, 4)).wait_recv()
    frecv[y] = fsend[y]
    feat_ref[...] = (
        frecv[0].astype(F32) + frecv[1].astype(F32) + frecv[2].astype(F32) + frecv[3].astype(F32)
    ).astype(BF)

    for k in range(1, 8):
        s3(rem(rep + k, 8), rem(rep + k, 8)).wait_recv()
    fin = jnp.sum(s3buf[...], axis=0)
    sc_ref[0] = jnp.sum(fin[1:2, :])
    sc_ref[1] = jnp.sum(fin[2:3, :])

    @pl.when(x < 3)
    def _():
        for k in range(1, 8):
            wz(rem(zl + k, 8), zl).wait_send()
        for k in (1, 2, 3):
            wx(rem(x + k, 4), x).wait_send()
    for k in (1, 2, 3):
        pass
        pcopy(rem(y + k, 4), y).wait_send()
        wy(rem(y + k, 4), y).wait_send()
        fcopy(rem(y + k, 4), y).wait_send()
        lcopy(rem(y + k, 4), y).wait_send()
    for k in (1, 2, 3):
        xcopy(rem(fst + k, 4), fst).wait_send()
    for n in range(3):
        @pl.when(snd != n)
        def _():
            ycopy(n, snd).wait_send()
    for k in range(4):
        pass
        wcc(k, c).wait_send()
        cchunk(k).wait_send()

    def body(slot, _):
        for h in (0, 1):
            t_sib(slot, h).wait_send()

            @pl.when((slot <= zl) & (zl < 7))
            def _():
                t_right(slot, h).wait_send()

            @pl.when((slot >= zl) & (zl > 0))
            def _():
                t_left(slot, h).wait_send()
        return 0
    lax.fori_loop(0, 8, body, 0)
    for k in range(1, 16):
        s2(rem(me2 + k, 16), me2).wait_send()
    for k in range(1, 8):
        s3(rem(rep + k, 8), rep).wait_send()

    @pl.when(snd < 3)
    def _():
        for k in range(1, 8):
            zcopy(rem(zl + k, 8), zl).wait_send()

    def body(k, _):
        @pl.when(jnp.logical_not(ag_from_self(k)))
        def _():
            acopy(0, rem(k, 2) * 3 + div(k, 4), rem(div(k, 2), 2)).wait_recv()
        return 0
    lax.fori_loop(0, 12, body, 0)
    for j in range(6):
        wg_ref[:, j * 128:(j + 1) * 128] = (abuf[0, j].astype(F32) + abuf[1, j].astype(F32))[0:12, :]

    @pl.when(snd < 3)
    def _():
        def body(k, _):
            @pl.when(jnp.logical_not(ag_self(k)))
            def _():
                acopy(k, me_a, zh).wait_send()
            return 0
        lax.fori_loop(0, 16, body, 0)


def hand_out(loss_in, feat_in, wg_in, sc_in, loss_out, feat_out, wg_out, sc_out):
    loss_out[...] = loss_in[...]
    feat_out[...] = feat_in[...]
    wg_out[...] = wg_in[...]
    sc_out[0] = sc_in[0]
    sc_out[1] = sc_in[1]


def per_device(pooled, text_embed, head_weight, natural_exponent_factor, logit_bias):
    vm = pl.BlockSpec(memory_space=pltpu.VMEM)
    sm = pl.BlockSpec(memory_space=pltpu.SMEM)
    V = pltpu.VMEM
    D = pltpu.SemaphoreType.DMA
    loss, feat, wgrad, sc = pl.pallas_call(
        kernel,
        out_shape=(
            jax.ShapeDtypeStruct((128,), F32),
            jax.ShapeDtypeStruct((128, 768), BF),
            jax.ShapeDtypeStruct((12, 768), F32),
            jax.ShapeDtypeStruct((2,), F32),
        ),
        in_specs=[vm, vm, vm, sm, sm],
        out_specs=(vm, vm, vm, sm),
        scratch_shapes=[
            V((8, 2, 128, 768), BF), V((4, 128, 768), BF), V((4, 2, 8, 16, 768), BF), V((4, 2, 96, 768), BF),
            V((768, 768), BF), V((1024, 768), BF), V((768, 768), BF), V((1024, 512), BF),
            V((512, 768), F32), V((512, 1), F32), V((512, 768), BF), V((512, 256), F32), V((512, 256), BF),
            V((512, 768), F32), V((512, 128), F32), V((2, 8, 128), F32),
            V((2, 512, 384), BF), V((4, 128, 768), BF), V((4, 128, 768), BF), V((2, 4, 8, 128), F32),
            V((4, 256, 384), BF), V((4, 256, 384), BF), V((4, 256, 384), BF), V((4, 256, 384), BF), V((3, 256, 128), BF), V((4, 256, 128), BF), V((256, 128), BF),
            V((2, 8, 16, 128), BF), V((8, 2, 16, 128), BF), V((2, 16, 128), BF), V((2, 6, 16, 128), BF),
            V((16, 8, 128), F32), V((8, 8, 128), F32),
            D((8, 2, 2)), D((8, 2)), D((8, 2)), D((8, 2)), D((4,)), D((4,)),
            D((8,)), D((8,)), D((4,)), D((4,)), D((4,)), D((4,)), D((4,)), D((4,)),
            D((4,)), D((4,)), D((4,)), D((4,)), D((4,)), D((4,)), D((4,)), D((4,)), D((4,)), D((4,)),
            D((8,)), D((8,)), D((2, 6)), D((16,)), D((16,)), D((16,)), D((8,)), D((8,)),
        ],
        compiler_params=pltpu.CompilerParams(
            collective_id=0, has_side_effects=True, vmem_limit_bytes=56 << 20
        ),
    )(pooled, text_embed, head_weight, natural_exponent_factor, logit_bias)
    return pl.pallas_call(
        hand_out,
        out_shape=(
            jax.ShapeDtypeStruct((128,), F32),
            jax.ShapeDtypeStruct((128, 768), BF),
            jax.ShapeDtypeStruct((12, 768), F32),
            jax.ShapeDtypeStruct((2,), F32),
        ),
        in_specs=[vm, vm, vm, sm],
        out_specs=(vm, vm, vm, sm),
    )(loss, feat, wgrad, sc)


def solution(mesh):
    return jax.shard_map(
        per_device,
        mesh=mesh,
        in_specs=(P(("rep", "zero"), None), P(("rep", "zero"), None), P("zero", None), P(), P()),
        out_specs=(P(("rep", "zero")), P(("rep", "zero"), None), P("zero", None), P()),
        check_vma=False,
    )
```

```python
import jax
import jax.numpy as jnp
from jax import lax
from jax.experimental import pallas as pl
from jax.experimental.pallas import tpu as pltpu
from jax.sharding import PartitionSpec as P

MESH = pl.DeviceIdType.MESH
F32 = jnp.float32
BF = jnp.bfloat16


def dev(x, zh, zl, y, c):
    return (x * 2 + zh, zl * 8 + y * 2 + c)


def rem(a, n):
    return lax.rem(a, jnp.int32(n))


def div(a, n):
    return lax.div(a, jnp.int32(n))


def nn(a, b):
    return jnp.dot(a, b, preferred_element_type=F32)


def nt(a, b):
    return lax.dot_general(a, b, (((1,), (1,)), ((), ())), preferred_element_type=F32)


def kernel(
    p_ref, t_ref, w_ref, nat_ref, bias_ref,
    loss_ref, feat_ref, wg_ref, sc_ref,
    txt, pool, wgat, w2, sel, selt, wc, pt, iu, inv, img, s_scr, slope_scr, acc, loss_acc, tot_acc,
    gp, fsend, frecv, lbuf, cs, cbuf, xs, xbuf, ys, ybuf, ysum, zs, zbuf, agb, abuf, s2buf, s3buf,
    t_rs, t_sr, t_sl, t_ss, p_rs, p_s, wz_rs, wz_s, wx_rs, wx_s, wy_rs, wy_s, wc_rs, wc_s,
    f_rs, f_s, l_rs, l_s, c_rs, c_s, x_rs, x_s, y_rs, y_s, z_rs, z_s, a_rs, a_s, s2_rs, s2_s, s3_rs, s3_s,
):
    rep = lax.axis_index("rep")
    zero = lax.axis_index("zero")
    x, zh = div(rep, 2), rem(rep, 2)
    zl, y, c = div(zero, 8), rem(div(zero, 2), 4), rem(zero, 2)
    oc = 1 - c
    temp = jnp.exp(jnp.full((8, 128), nat_ref[0], F32))[0:1, 0:1]
    bias = bias_ref[0]

    def rc(src, dst, ss, rs, to):
        return pltpu.make_async_remote_copy(src, dst, ss, rs, device_id=to, device_id_type=MESH)

    bar = pltpu.get_barrier_semaphore()

    def sig(to):
        pl.semaphore_signal(bar, inc=1, device_id=to, device_id_type=MESH)

    wgat[y, c, zl] = jnp.zeros((16, 768), BF)
    wgat[y, c, zl, 0:12] = w_ref[...]
    sig(dev(x, zh, zl, y, oc))
    for k in (1, 2, 3):
        sig(dev(x, zh, zl, rem(y + k, 4), c))
        sig(dev(rem(x + k, 4), zh, zl, y, c))
        sig(dev(rem(x + k, 4), 1 - zh, zl, y, c))
    for k in range(1, 8):
        sig(dev(x, zh, rem(zl + k, 8), y, c))
    sig(dev(x, 1 - zh, zl, y, c))

    tf = t_ref[...].astype(F32)
    txt[zl, c] = (tf * lax.rsqrt(jnp.sum(tf * tf, axis=1, keepdims=True) + 1e-06)).astype(BF)
    pl.semaphore_wait(bar, 18)

    def tpiece(slot, cc, h):
        return txt.at[slot, cc, pl.ds(h * 64, 64)]

    def t_right(slot, h):
        return rc(tpiece(slot, c, h), tpiece(slot, c, h), t_sr.at[slot, h], t_rs.at[slot, c, h], dev(x, zh, zl + 1, y, c))

    def t_left(slot, h):
        return rc(tpiece(slot, c, h), tpiece(slot, c, h), t_sl.at[slot, h], t_rs.at[slot, c, h], dev(x, zh, zl - 1, y, c))

    def t_sib(slot, h):
        return rc(tpiece(slot, c, h), tpiece(slot, c, h), t_ss.at[slot, h], t_rs.at[slot, c, h], dev(x, zh, zl, y, oc))

    def t_wait(slot, cc, h):
        rc(tpiece(slot, cc, h), tpiece(slot, cc, h), t_ss.at[slot, h], t_rs.at[slot, cc, h], dev(x, zh, zl, y, oc)).wait_recv()

    def wz(k_to, slot):
        piece = wgat.at[y, c, slot, :, pl.ds(pl.multiple_of(x * 256, 256), 256)]
        return rc(piece, piece, wz_s.at[k_to], wz_rs.at[slot], dev(x, zh, k_to, y, c))

    def wx(xt, slot):
        piece = wgat.at[y, c, :, :, pl.ds(pl.multiple_of(slot * 256, 256), 256)]
        return rc(piece, piece, wx_s.at[xt], wx_rs.at[slot], dev(xt, zh, zl, y, c))

    def pcopy(yt, slot):
        return rc(p_ref, pool.at[slot], p_s.at[yt], p_rs.at[slot], dev(x, zh, zl, yt, c))

    @pl.when(x < 3)
    def _():
        for k in range(1, 8):
            wz(rem(zl + k, 8), zl).start()
    for h in (0, 1):
        @pl.when(zl < 7)
        def _():
            t_right(zl, h).start()

        @pl.when(zl > 0)
        def _():
            t_left(zl, h).start()
    for h in (0, 1):
        t_sib(zl, h).start()

    for k in (1, 3, 2):
        pcopy(rem(y + k, 4), y).start()

    def forward(d):
        pass
        for h in (0, 1):
            @pl.when(zl - d >= 0)
            def _():
                t_wait(zl - d, c, h)

                @pl.when(zl < 7)
                def _():
                    t_right(zl - d, h).start()
                t_sib(zl - d, h).start()

            @pl.when(zl + d <= 7)
            def _():
                t_wait(zl + d, c, h)

                @pl.when(zl > 0)
                def _():
                    t_left(zl + d, h).start()
                t_sib(zl + d, h).start()

    pool[y] = p_ref[...]

    def where_row(k):
        r = k % 16
        return jnp.where(r < 12, 96 * ((k // 16) % 8) + 12 * (k // 128) + r, -1)

    slots = lax.broadcasted_iota(jnp.int32, (1, 128), 1)
    slots = jnp.where(slots % 16 < 12, 12 * (slots // 16) + slots % 16, -1)
    csel = jnp.where(lax.broadcasted_iota(jnp.int32, (96, 1), 0) == slots, 1.0, 0.0).astype(BF)
    cols = lax.broadcasted_iota(jnp.int32, (1, 768), 1)
    cols = 96 * ((cols % 96) // 12) + 12 * (cols // 96) + cols % 12

    def body(i, _):
        rows = lax.broadcasted_iota(jnp.int32, (128, 1), 0) + i * 128
        sel[pl.ds(i * 128, 128), :] = jnp.where(rows == cols, 1.0, 0.0).astype(BF)
        return 0
    lax.fori_loop(0, 6, body, 0)
    lanes = lax.broadcasted_iota(jnp.int32, (1, 768), 1)

    def body(i, _):
        rows = where_row(lax.broadcasted_iota(jnp.int32, (128, 1), 0) + i * 128)
        selt[pl.ds(i * 128, 128), :] = jnp.where(rows == lanes, 1.0, 0.0).astype(BF)
        return 0
    lax.fori_loop(0, 8, body, 0)
    acc[...] = jnp.zeros_like(acc)
    loss_acc[...] = jnp.zeros_like(loss_acc)
    tot_acc[...] = jnp.zeros_like(tot_acc)
    @pl.when(x < 3)
    def _():
        for k in (1, 7, 2, 6, 3, 5, 4):
            wz(rem(zl + k, 8), rem(zl + k, 8)).wait_recv()
        for k in (1, 3, 2):
            wx(rem(x + k, 4), x).start()

    def wy(yt, slot):
        return rc(w2.at[slot, c], w2.at[slot, c], wy_s.at[yt], wy_rs.at[slot], dev(x, zh, zl, yt, c))

    def wcc(slot, cc):
        return rc(w2.at[slot, cc], w2.at[slot, cc], wc_s.at[slot], wc_rs.at[slot], dev(x, zh, zl, y, oc))

    forward(1)
    for k in range(3):
        @pl.when(x != k)
        def _():
            wx(0, k).wait_recv()
    w2[y, c] = nn(csel, wgat[y, c].reshape(128, 768)).astype(BF)
    for k in (1, 3, 2):
        wy(rem(y + k, 4), y).start()
    wcc(y, c).start()
    forward(2)
    for k in (1, 3, 2):
        pcopy(rem(y + k, 4), rem(y + k, 4)).wait_recv()

    def body(i, _):
        pt[pl.ds(i * 256, 256), :] = nt(selt[pl.ds(i * 256, 256), :], pool[...].reshape(512, 768)).astype(BF)
        return 0
    lax.fori_loop(0, 4, body, 0)
    forward(3)
    for k in (1, 3, 2):
        wy(rem(y + k, 4), rem(y + k, 4)).wait_recv()
        wcc(rem(y + k, 4), c).start()
    for k in (0, 1, 3, 2):
        wcc(rem(y + k, 4), oc).wait_recv()

    def body(i, _):
        wc[pl.ds(i * 256, 256), :] = nn(sel[pl.ds(i * 256, 256), :], w2[...].reshape(768, 768)).astype(BF)
        return 0
    lax.fori_loop(0, 3, body, 0)
    for n in range(3):
        iu[:, n * 256:(n + 1) * 256] = nn(pool[...].reshape(512, 768), wc[:, n * 256:(n + 1) * 256])

    def body(i, _):
        rows = pl.ds(i * 64, 64)
        pr = iu[rows, :]
        iv = lax.rsqrt(jnp.sum(pr * pr, axis=1, keepdims=True) + 1e-06)
        un = pr * iv
        iu[rows, :] = un
        inv[rows, :] = iv
        img[rows, :] = un.astype(BF)
        return 0
    lax.fori_loop(0, 8, body, 0)

    def compute(slot, own):
        pass
        for h in (0, 1):
            t_wait(slot, oc, h)
        tt = txt[slot].reshape(256, 768)
        s_scr[...] = nt(img[...], tt)

        def body(i, _):
            rows = pl.ds(i * 64, 64)
            scaled = s_scr[rows, :] * temp
            logit = scaled + bias
            if own:
                diag = (
                    lax.broadcasted_iota(jnp.int32, (64, 256), 0) + (i * 64 - y * 128)
                    == lax.broadcasted_iota(jnp.int32, (64, 256), 1) - c * 128
                ) & (lax.broadcasted_iota(jnp.int32, (64, 256), 1) // 128 == c)
                m = jnp.where(diag, -logit, logit)
            else:
                m = logit
            e = jnp.exp(-jnp.abs(m))
            u = 1.0 + e
            rcp = 1.0 / u
            lg = jnp.log(u) + (e - (u - 1.0)) * rcp
            soft = jnp.maximum(m, 0.0) + lg
            slope = jnp.where(m >= 0.0, 1.0, e) * rcp
            if own:
                slope = jnp.where(diag, -slope, slope)
            loss_acc[rows, :] += soft[:, 0:128] + soft[:, 128:256]
            sl = slope[:, 0:128] + slope[:, 128:256]
            st = slope * scaled
            st = st[:, 0:128] + st[:, 128:256]
            tot_acc[0] += jnp.sum(st.reshape(8, 8, 128), axis=0)
            tot_acc[1] += jnp.sum(sl.reshape(8, 8, 128), axis=0)
            slope_scr[rows, :] = slope.astype(BF)
            return 0
        lax.fori_loop(0, 8, body, 0)
        for n in range(3):
            acc[:, n * 256:(n + 1) * 256] += nn(slope_scr[...], tt[:, n * 256:(n + 1) * 256])

    compute(zl, True)
    forward(4)

    def both(d):
        def body(side, _):
            slot = zl + d * (2 * side - 1)

            @pl.when((slot >= 0) & (slot <= 7))
            def _():
                compute(slot, False)
            return 0
        lax.fori_loop(0, 2, body, 0)

    def body(d, _):
        @pl.when((d == 2) | (d == 4) | (d == 7))
        def _():
            forward(jnp.where(d == 2, 5, jnp.where(d == 4, 6, 7)))
        both(d)
        return 0
    lax.fori_loop(1, 8, body, 0)

    def body(i, _):
        rows = pl.ds(i * 64, 64)
        gu = acc[rows, :] * temp
        un = iu[rows, :]
        g = ((gu - un * jnp.sum(un * gu, axis=1, keepdims=True)) * inv[rows, :]).astype(BF)
        gp[0, rows, :] = g[:, 0:384]
        gp[1, rows, :] = g[:, 384:768]
        return 0
    lax.fori_loop(0, 8, body, 0)
    def cchunk(j):
        return rc(cs.at[j], cbuf.at[j], c_s.at[j], c_rs.at[j], dev(x, zh, zl, y, oc))

    def body(k, _):
        j = rem(jnp.where(c == 0, y, x) + k, 4)
        cs[j] = nn(pt[pl.ds(j * 256, 256), :], gp[oc]).astype(BF)
        cchunk(j).start()
        return 0
    lax.fori_loop(1, 5, body, 0)

    def zcopy(to, slot):
        return rc(zs.at[:, to], zbuf.at[slot], z_s.at[to], z_rs.at[slot], dev(x, zh, to, y, c))

    fst, snd = jnp.where(c == 0, x, y), jnp.where(c == 0, y, x)

    def place(f, g):
        return dev(jnp.where(c == 0, f, g), zh, zl, jnp.where(c == 0, g, f), c)

    def xcopy(to, slot):
        return rc(xs.at[to], xbuf.at[slot], x_s.at[to], x_rs.at[slot], place(to, snd))

    def ycopy(to, slot):
        return rc(ys.at[to], ybuf.at[slot], y_s.at[to], y_rs.at[slot], place(fst, to))

    def body(k, _):
        j = rem(fst + k, 4)
        mine = nn(pt[pl.ds(j * 256, 256), :], gp[c])
        cchunk(j).wait_recv()
        xs[j] = (mine + cbuf[j].astype(F32)).astype(BF)

        @pl.when(k < 4)
        def _():
            xcopy(j, fst).start()
        return 0
    lax.fori_loop(1, 5, body, 0)
    xbuf[fst] = xs[fst]

    for n in range(3):
        blk = wc[n * 256:(n + 1) * 256, :]
        fsend[:, :, n * 256:(n + 1) * 256] = (
            (nt(gp[0], blk[:, 0:384]) + nt(gp[1], blk[:, 384:768])).astype(BF).reshape(4, 128, 256)
        )

    def fcopy(yt, slot):
        return rc(fsend.at[yt], frecv.at[slot], f_s.at[yt], f_rs.at[slot], dev(x, zh, zl, yt, c))

    row = lax.broadcasted_iota(jnp.int32, (8, 128), 0)
    tl = jnp.sum(tot_acc[0], axis=0, keepdims=True)
    bl = jnp.sum(tot_acc[1], axis=0, keepdims=True)
    for j in range(4):
        part = jnp.sum(loss_acc[j * 128:(j + 1) * 128, :].T, axis=0, keepdims=True)
        lbuf[0, j] = jnp.where(row == 0, part, jnp.where(row == 1, tl, jnp.where(row == 2, bl, 0.0)))

    def lcopy(yt, slot):
        return rc(lbuf.at[0, yt], lbuf.at[1, slot], l_s.at[yt], l_rs.at[slot], dev(x, zh, zl, yt, c))

    for k in (1, 2, 3):
        lcopy(rem(y + k, 4), y).start()
    lbuf[1, y] = lbuf[0, y]
    for k in (1, 2, 3):
        lcopy(rem(y + k, 4), rem(y + k, 4)).wait_recv()
    ltot = lbuf[1, 0] + lbuf[1, 1] + lbuf[1, 2] + lbuf[1, 3]
    loss_ref[...] = ltot[0]
    me2 = zl * 2 + c
    s2buf[me2] = ltot

    def s2(to, slot):
        return rc(s2buf.at[me2], s2buf.at[slot], s2_s.at[to], s2_rs.at[slot], dev(x, zh, div(to, 2), y, rem(to, 2)))

    for k in range(1, 16):
        s2(rem(me2 + k, 16), me2).start()

    for k in (1, 3, 2):
        xcopy(0, rem(fst + k, 4)).wait_recv()

    def body(i, _):
        rows = pl.ds(i * 64, 64)
        part = xbuf[0, rows, :].astype(F32)
        for k in range(1, 4):
            part = part + xbuf[k, rows, :].astype(F32)
        for n in range(3):
            ys[n, rows, :] = part[:, n * 128:(n + 1) * 128].astype(BF)
        return 0
    lax.fori_loop(0, 4, body, 0)
    for n in range(3):
        @pl.when(snd != n)
        def _():
            ycopy(n, snd).start()
    for k in (2, 1, 3):
        fcopy(rem(y + k, 4), y).start()

    @pl.when(snd < 3)
    def _():
        ybuf[snd] = ys[snd]
        for k in (1, 3, 2):
            ycopy(0, rem(snd + k, 4)).wait_recv()
        ysum[...] = (
            ybuf[0].astype(F32) + ybuf[1].astype(F32) + ybuf[2].astype(F32) + ybuf[3].astype(F32)
        ).astype(BF)
        zs[...] = ysum[...].reshape(2, 8, 16, 128)
        for k in (4, 3, 5, 2, 6, 1, 7):
            zcopy(rem(zl + k, 8), zl).start()


    for k in range(1, 16):
        s2(rem(me2 + k, 16), rem(me2 + k, 16)).wait_recv()
    s3buf[rep] = jnp.sum(s2buf[...], axis=0)

    def s3(to, slot):
        return rc(s3buf.at[rep], s3buf.at[slot], s3_s.at[to], s3_rs.at[slot], (to, zero))

    for k in range(1, 8):
        s3(rem(rep + k, 8), rep).start()

    def ag_self(k):
        return (div(k, 4) == x) & (rem(div(k, 2), 2) == zh) & (fst == y) & (rem(k, 2) == c)

    def ag_from_self(k):
        return (fst == y) & (div(k, 4) == snd) & (rem(div(k, 2), 2) == zh) & (rem(k, 2) == c)

    def acopy(k, j, h):
        return rc(
            agb.at[rem(k, 2)], abuf.at[h, j], a_s.at[k], a_rs.at[h, j],
            dev(div(k, 4), rem(div(k, 2), 2), zl, fst, rem(k, 2)),
        )

    me_a = c * 3 + snd

    @pl.when(snd < 3)
    def _():
        zbuf[zl] = zs[:, zl]
        for k in (1, 7, 2, 6, 3, 5, 4):
            zcopy(rem(zl + k, 8), rem(zl + k, 8)).wait_recv()
        agb[...] = jnp.sum(zbuf[...].astype(F32), axis=0).astype(BF)

        def body(k, _):
            @pl.when(jnp.logical_not(ag_self(k)))
            def _():
                acopy(k, me_a, zh).start()
            return 0
        lax.fori_loop(0, 16, body, 0)

        @pl.when(fst == y)
        def _():
            abuf[zh, me_a] = agb[c]

    for k in (1, 3, 2):
        fcopy(rem(y + k, 4), rem(y + k, 4)).wait_recv()
    frecv[y] = fsend[y]
    feat_ref[...] = (
        frecv[0].astype(F32) + frecv[1].astype(F32) + frecv[2].astype(F32) + frecv[3].astype(F32)
    ).astype(BF)

    for k in range(1, 8):
        s3(rem(rep + k, 8), rem(rep + k, 8)).wait_recv()
    fin = jnp.sum(s3buf[...], axis=0)
    sc_ref[0] = jnp.sum(fin[1:2, :])
    sc_ref[1] = jnp.sum(fin[2:3, :])

    @pl.when(x < 3)
    def _():
        for k in range(1, 8):
            wz(rem(zl + k, 8), zl).wait_send()
        for k in (1, 2, 3):
            wx(rem(x + k, 4), x).wait_send()
    for k in (1, 2, 3):
        pass
        pcopy(rem(y + k, 4), y).wait_send()
        wy(rem(y + k, 4), y).wait_send()
        fcopy(rem(y + k, 4), y).wait_send()
        lcopy(rem(y + k, 4), y).wait_send()
    for k in (1, 2, 3):
        xcopy(rem(fst + k, 4), fst).wait_send()
    for n in range(3):
        @pl.when(snd != n)
        def _():
            ycopy(n, snd).wait_send()
    for k in range(4):
        pass
        wcc(k, c).wait_send()
        cchunk(k).wait_send()

    def body(slot, _):
        for h in (0, 1):
            t_sib(slot, h).wait_send()

            @pl.when((slot <= zl) & (zl < 7))
            def _():
                t_right(slot, h).wait_send()

            @pl.when((slot >= zl) & (zl > 0))
            def _():
                t_left(slot, h).wait_send()
        return 0
    lax.fori_loop(0, 8, body, 0)
    for k in range(1, 16):
        s2(rem(me2 + k, 16), me2).wait_send()
    for k in range(1, 8):
        s3(rem(rep + k, 8), rep).wait_send()

    @pl.when(snd < 3)
    def _():
        for k in range(1, 8):
            zcopy(rem(zl + k, 8), zl).wait_send()

    def body(k, _):
        @pl.when(jnp.logical_not(ag_from_self(k)))
        def _():
            acopy(0, rem(k, 2) * 3 + div(k, 4), rem(div(k, 2), 2)).wait_recv()
        return 0
    lax.fori_loop(0, 12, body, 0)
    for j in range(6):
        wg_ref[:, j * 128:(j + 1) * 128] = (abuf[0, j].astype(F32) + abuf[1, j].astype(F32))[0:12, :]

    @pl.when(snd < 3)
    def _():
        def body(k, _):
            @pl.when(jnp.logical_not(ag_self(k)))
            def _():
                acopy(k, me_a, zh).wait_send()
            return 0
        lax.fori_loop(0, 16, body, 0)


def hand_out(loss_in, feat_in, wg_in, sc_in, loss_out, feat_out, wg_out, sc_out):
    loss_out[...] = loss_in[...]
    feat_out[...] = feat_in[...]
    wg_out[...] = wg_in[...]
    sc_out[0] = sc_in[0]
    sc_out[1] = sc_in[1]


def per_device(pooled, text_embed, head_weight, natural_exponent_factor, logit_bias):
    vm = pl.BlockSpec(memory_space=pltpu.VMEM)
    sm = pl.BlockSpec(memory_space=pltpu.SMEM)
    V = pltpu.VMEM
    D = pltpu.SemaphoreType.DMA
    loss, feat, wgrad, sc = pl.pallas_call(
        kernel,
        out_shape=(
            jax.ShapeDtypeStruct((128,), F32),
            jax.ShapeDtypeStruct((128, 768), BF),
            jax.ShapeDtypeStruct((12, 768), F32),
            jax.ShapeDtypeStruct((2,), F32),
        ),
        in_specs=[vm, vm, vm, sm, sm],
        out_specs=(vm, vm, vm, sm),
        scratch_shapes=[
            V((8, 2, 128, 768), BF), V((4, 128, 768), BF), V((4, 2, 8, 16, 768), BF), V((4, 2, 96, 768), BF),
            V((768, 768), BF), V((1024, 768), BF), V((768, 768), BF), V((1024, 512), BF),
            V((512, 768), F32), V((512, 1), F32), V((512, 768), BF), V((512, 256), F32), V((512, 256), BF),
            V((512, 768), F32), V((512, 128), F32), V((2, 8, 128), F32),
            V((2, 512, 384), BF), V((4, 128, 768), BF), V((4, 128, 768), BF), V((2, 4, 8, 128), F32),
            V((4, 256, 384), BF), V((4, 256, 384), BF), V((4, 256, 384), BF), V((4, 256, 384), BF), V((3, 256, 128), BF), V((4, 256, 128), BF), V((256, 128), BF),
            V((2, 8, 16, 128), BF), V((8, 2, 16, 128), BF), V((2, 16, 128), BF), V((2, 6, 16, 128), BF),
            V((16, 8, 128), F32), V((8, 8, 128), F32),
            D((8, 2, 2)), D((8, 2)), D((8, 2)), D((8, 2)), D((4,)), D((4,)),
            D((8,)), D((8,)), D((4,)), D((4,)), D((4,)), D((4,)), D((4,)), D((4,)),
            D((4,)), D((4,)), D((4,)), D((4,)), D((4,)), D((4,)), D((4,)), D((4,)), D((4,)), D((4,)),
            D((8,)), D((8,)), D((2, 6)), D((16,)), D((16,)), D((16,)), D((8,)), D((8,)),
        ],
        compiler_params=pltpu.CompilerParams(
            collective_id=0, has_side_effects=True, vmem_limit_bytes=56 << 20
        ),
    )(pooled, text_embed, head_weight, natural_exponent_factor, logit_bias)
    return pl.pallas_call(
        hand_out,
        out_shape=(
            jax.ShapeDtypeStruct((128,), F32),
            jax.ShapeDtypeStruct((128, 768), BF),
            jax.ShapeDtypeStruct((12, 768), F32),
            jax.ShapeDtypeStruct((2,), F32),
        ),
        in_specs=[vm, vm, vm, sm],
        out_specs=(vm, vm, vm, sm),
    )(loss, feat, wgrad, sc)


def solution(mesh):
    return jax.shard_map(
        per_device,
        mesh=mesh,
        in_specs=(P(("rep", "zero"), None), P(("rep", "zero"), None), P("zero", None), P(), P()),
        out_specs=(P(("rep", "zero")), P(("rep", "zero"), None), P("zero", None), P()),
        check_vma=False,
    )
```
